32 devices in a mesh: row: 8 (over z, y), col: 4 (over x, core).
Axes of the slice: x: 2, y: 2, z: 4, core: 2. Of those that a mesh axis runs over, the one named last changes fastest.
Arguments:
- a_weights: bfloat16 [4096, 1024], P('row', 'col'), may hold values from 0.0001 to 1, as said below
- tile_mask: int32 [8, 2], replicated, may hold values from 0 to 1, as said below
- pair_mask: int32 [8, 8], replicated, may hold values from 0 to 1, as said below
Outputs:
- jaccard: bfloat16 [4096, 4096], P('row', 'col')
The draws below stay inside these ranges and needn't reach their ends.
Inputs may be any that keep to these rules, and one draw needn't show every extreme that they name: `a_weights`: all weights positive. `tile_mask`: 1 where a tile is present; tile (I, I mod 2) of every block row I is present. `pair_mask`: symmetric, with ones on the diagonal.
All inputs are finite; a program needn't handle non-finite values.
Results may differ from the reference program's by a relative error of at most 0.001.
Values may be sent and summed in bfloat16 or wider, within the bound.
A program may use at most 64 MiB of HBM per device.

```python
import math
import jax
import jax.numpy as jnp
from jax import lax

BLOCK = 512
NEIGH_BLOCKS = 2
CELLS = 4096
NEIGH = 1024
ROW_BLOCKS = 8


def draw_a_weights(key, part):
    key_base = jax.random.fold_in(key, 0)
    values = jnp.exp(jax.random.uniform(key_base, (CELLS, NEIGH), jnp.float32, math.log(0.001), 0.0))
    return values.astype(jnp.bfloat16)


def draw_tile_mask(key, part):
    flags = jax.random.randint(key, (ROW_BLOCKS, NEIGH_BLOCKS), 0, 2).astype(jnp.int32)
    forced = jnp.arange(NEIGH_BLOCKS)[None, :] == (jnp.arange(ROW_BLOCKS) % NEIGH_BLOCKS)[:, None]
    return jnp.maximum(flags, forced.astype(jnp.int32)).astype(jnp.int32)


def draw_pair_mask(key, part):
    flags = jax.random.randint(key, (ROW_BLOCKS, ROW_BLOCKS), 0, 2).astype(jnp.int32)
    upper = jnp.triu(flags, 1)
    return (upper + upper.T + jnp.eye(ROW_BLOCKS, dtype=jnp.int32)).astype(jnp.int32)


def setup_inputs(seed: int = 0) -> dict:
    seeds = jax.random.split(jax.random.key(seed), 4)
    return {
        "a_weights": draw_a_weights(jax.random.fold_in(seeds[3], 71), 0),
        "tile_mask": draw_tile_mask(jax.random.fold_in(seeds[3], 71), 0),
        "pair_mask": draw_pair_mask(jax.random.fold_in(seeds[3], 71), 0),
    }


def reference(a_weights, tile_mask, pair_mask):
    tiles = a_weights.reshape(ROW_BLOCKS, BLOCK, NEIGH_BLOCKS, BLOCK)
    masked = tiles * tile_mask.astype(jnp.bfloat16)[:, None, :, None]
    graph = masked.reshape(CELLS, NEIGH)
    degree = jnp.sum(jnp.square(graph.astype(jnp.float32)), axis=1)
    col_open = jnp.repeat(pair_mask, BLOCK, axis=1) > 0

    def one_block(inputs):
        block_rows, block_degree, open_row = inputs
        shared = jnp.dot(block_rows, graph.T, preferred_element_type=jnp.float32)
        weights = shared / (block_degree[:, None] + degree[None, :] - shared)
        return jnp.where(open_row[None, :], weights, jnp.zeros_like(weights)).astype(jnp.bfloat16)

    blocks = lax.map(one_block, (graph.reshape(ROW_BLOCKS, BLOCK, NEIGH), degree.reshape(ROW_BLOCKS, BLOCK), col_open))
    return blocks.reshape(CELLS, CELLS)
```

```python
import functools

import jax
import jax.numpy as jnp
from jax import lax
from jax.experimental import pallas as pl
from jax.experimental.pallas import tpu as pltpu
from jax.sharding import PartitionSpec as P

BLOCK = 512
PIECES = 2
MESH = pl.DeviceIdType.MESH
UP, DOWN, SIDE, CORE = range(4)


def kernel(rows, cols, tile_ref, pair_ref, a_ref, out_ref, buf, send_x, send, recv):
    levels, chips = rows // 2, cols // 2
    width = a_ref.shape[1]
    part = BLOCK // PIECES
    row, col = lax.axis_index("row"), lax.axis_index("col")
    z, y = row // 2, row % 2
    q, k = col // 2, col % 2
    near = z // 2 == q
    slot = jnp.where(near, 2 * (z - 2 * q) + y, 4)

    flag = tile_ref[row, (col * width) // BLOCK]
    own = a_ref[...]
    buf[slot, col] = jnp.where(flag > 0, own, jnp.zeros_like(own))

    up_id, down_id = (row + 2, col), (row - 2, col)
    side_id, core_id = (row + 1 - 2 * y, col), (row, col + 1 - 2 * k)
    x_ids = [(row, lax.rem(col + 2 * i, cols)) for i in range(1, chips)]
    has_up, has_down = z + 1 < levels, z > 0

    barrier = pltpu.get_barrier_semaphore()
    for device in [side_id, core_id] + x_ids:
        pl.semaphore_signal(barrier, inc=1, device_id=device, device_id_type=MESH)
    for there, device in ((has_up, up_id), (has_down, down_id)):

        @pl.when(there)
        def _():
            pl.semaphore_signal(barrier, inc=1, device_id=device, device_id_type=MESH)

    pl.semaphore_wait(
        barrier, chips + 1 + has_up.astype(jnp.int32) + has_down.astype(jnp.int32)
    )

    sent = []

    def copy(kind, j, s, p, device):
        ref = buf.at[j, 2 * s + k, pl.ds(p * part, part), :]
        return pltpu.make_async_remote_copy(
            src_ref=ref, dst_ref=ref, send_sem=send.at[kind, j, s, p],
            recv_sem=recv.at[j, 2 * s + k, p], device_id=device, device_id_type=MESH)

    def start(when, kind, j, s, p, device):
        made = copy(kind, j, s, p, device)
        sent.append((when, made))
        if when is None:
            made.start()
        else:
            pl.when(when)(made.start)

    def arrived(j, s, parity, p):
        ref = buf.at[j, 2 * s + parity, pl.ds(p * part, part), :]
        pltpu.make_async_remote_copy(
            src_ref=ref, dst_ref=ref, send_sem=send.at[CORE, j, s, p],
            recv_sem=recv.at[j, 2 * s + parity, p], device_id=core_id,
            device_id_type=MESH).wait_recv()

    for p in range(PIECES):
        for i, device in enumerate(x_ids):
            other = device[1] // 2
            there = jnp.where(z // 2 == other, 2 * (z - 2 * other) + y, 4)
            made = pltpu.make_async_remote_copy(
                src_ref=buf.at[slot, col, pl.ds(p * part, part), :],
                dst_ref=buf.at[there, col, pl.ds(p * part, part), :],
                send_sem=send_x.at[i, p], recv_sem=recv.at[there, col, p],
                device_id=device, device_id_type=MESH)
            sent.append((None, made))
            made.start()

    def from_side(a, s, p):
        j = 2 * a + 1 - y
        arrived(j, s, k, p)
        start(a == 1 - k, CORE, j, s, p, core_id)

    far_first = (z > 2 * q).astype(jnp.int32)
    items = [
        (far_first if a == 0 else 1 - far_first, i, p)
        for a in range(2) for i in range(chips) for p in range(PIECES)
    ]
    before = []
    for a, i, p in items:
        s = lax.rem(q + i, chips)
        j = 2 * a + y
        here = z == 2 * q + a
        if i == 0:
            pl.when(jnp.logical_not(here))(functools.partial(arrived, j, s, k, p))
        else:
            arrived(j, s, k, p)
        start(has_up & (z >= 2 * q + a), UP, j, s, p, up_id)
        start(has_down & (z <= 2 * q + a), DOWN, j, s, p, down_id)
        start(None, SIDE, j, s, p, side_id)
        start(here | (a == 1 - k), CORE, j, s, p, core_id)
        before.append((a, s, p))
        if len(before) > 2:
            from_side(*before.pop(0))
    for args in before:
        from_side(*args)

    far = jnp.logical_not(near)
    for i in range(chips):
        for p in range(PIECES):
            s = lax.rem(q + i, chips)
            if i > 0:
                pl.when(far)(functools.partial(arrived, 4, s, k, p))
            start(far, CORE, 4, s, p, core_id)
    for s in range(chips):
        for p in range(PIECES):
            arrived(slot, s, 1 - k, p)
            for other in range(2):
                j = 2 * k + other
                pl.when(j != slot)(functools.partial(arrived, j, s, 1 - k, p))

    ones = jnp.ones((8, width), jnp.bfloat16)
    dims = (((1,), (1,)), ((), ()))
    row_degree = jnp.zeros((BLOCK, 1), jnp.float32)
    for s in range(cols):
        mine = buf[slot, s].astype(jnp.float32)
        row_degree += jnp.sum(mine * mine, axis=1, keepdims=True)
    for other in range(2):
        j = 2 * k + other
        open_pair = pair_ref[row, 2 * col + other] > 0
        for p in range(PIECES):
            shared = jnp.zeros((BLOCK, part), jnp.float32)
            degree = jnp.zeros((8, part), jnp.float32)
            for s in range(cols):
                theirs = buf[j, s, p * part:(p + 1) * part, :]
                shared += lax.dot_general(
                    buf[slot, s], theirs, dims, preferred_element_type=jnp.float32)
                wide = theirs.astype(jnp.float32)
                square = wide * wide
                high = square.astype(jnp.bfloat16)
                low = (square - high.astype(jnp.float32)).astype(jnp.bfloat16)
                degree += lax.dot_general(ones, high, dims, preferred_element_type=jnp.float32)
                degree += lax.dot_general(ones, low, dims, preferred_element_type=jnp.float32)
            weights = shared / (row_degree + degree[:1] - shared)
            weights = jnp.where(open_pair, weights, jnp.zeros_like(weights))
            first = other * BLOCK + p * part
            out_ref[:, first:first + part] = weights.astype(jnp.bfloat16)

    for when, made in sent:
        if when is None:
            made.wait_send()
        else:
            pl.when(when)(made.wait_send)


def body(rows, cols, a_weights, tile_mask, pair_mask):
    width = a_weights.shape[1]
    chips = cols // 2
    return pl.pallas_call(
        functools.partial(kernel, rows, cols),
        out_shape=jax.ShapeDtypeStruct((BLOCK, rows // cols * BLOCK), jnp.bfloat16),
        in_specs=[
            pl.BlockSpec(memory_space=pltpu.SMEM),
            pl.BlockSpec(memory_space=pltpu.SMEM),
            pl.BlockSpec(memory_space=pltpu.VMEM),
        ],
        out_specs=pl.BlockSpec(memory_space=pltpu.VMEM),
        scratch_shapes=[
            pltpu.VMEM((5, cols, BLOCK, width), jnp.bfloat16),
            pltpu.SemaphoreType.DMA((chips - 1, PIECES)),
            pltpu.SemaphoreType.DMA((4, 5, chips, PIECES)),
            pltpu.SemaphoreType.DMA((5, cols, PIECES)),
        ],
        compiler_params=pltpu.CompilerParams(
            collective_id=0, has_side_effects=True, vmem_limit_bytes=40 * 2**20),
        cost_estimate=pl.CostEstimate(
            flops=4 * BLOCK * BLOCK * width * cols, bytes_accessed=4 * BLOCK * BLOCK,
            transcendentals=0),
    )(tile_mask, pair_mask, a_weights)


def solution(mesh):
    rows, cols = mesh.shape["row"], mesh.shape["col"]
    in_specs = (P("row", "col"), P(), P())
    out_specs = P("row", "col")
    return jax.shard_map(
        functools.partial(body, rows, cols), mesh=mesh, in_specs=in_specs,
        out_specs=out_specs, check_vma=False)
```

```python
import functools

import jax
import jax.numpy as jnp
from jax import lax
from jax.experimental import pallas as pl
from jax.experimental.pallas import tpu as pltpu
from jax.sharding import PartitionSpec as P

BLOCK = 512
PIECES = 4
LAG = 4
MESH = pl.DeviceIdType.MESH
UP, DOWN, SIDE, CORE = range(4)


def kernel(rows, cols, tile_ref, pair_ref, a_ref, out_ref, buf, send_x, send, recv):
    levels, chips = rows // 2, cols // 2
    width = a_ref.shape[1]
    part = BLOCK // PIECES
    row, col = lax.axis_index("row"), lax.axis_index("col")
    z, y = row // 2, row % 2
    q, k = col // 2, col % 2
    near = z // 2 == q
    slot = jnp.where(near, 2 * (z - 2 * q) + y, 4)

    flag = tile_ref[row, (col * width) // BLOCK]
    own = a_ref[...]
    buf[slot, col] = jnp.where(flag > 0, own, jnp.zeros_like(own))

    up_id, down_id = (row + 2, col), (row - 2, col)
    side_id, core_id = (row + 1 - 2 * y, col), (row, col + 1 - 2 * k)
    x_ids = [(row, lax.rem(col + 2 * i, cols)) for i in range(1, chips)]
    has_up, has_down = z + 1 < levels, z > 0

    barrier = pltpu.get_barrier_semaphore()
    for device in [side_id, core_id] + x_ids:
        pl.semaphore_signal(barrier, inc=1, device_id=device, device_id_type=MESH)
    for there, device in ((has_up, up_id), (has_down, down_id)):

        @pl.when(there)
        def _():
            pl.semaphore_signal(barrier, inc=1, device_id=device, device_id_type=MESH)

    pl.semaphore_wait(
        barrier, chips + 1 + has_up.astype(jnp.int32) + has_down.astype(jnp.int32)
    )

    sent = []

    def copy(kind, j, s, p, device):
        ref = buf.at[j, 2 * s + k, pl.ds(p * part, part), :]
        return pltpu.make_async_remote_copy(
            src_ref=ref, dst_ref=ref, send_sem=send.at[kind, j, s, p],
            recv_sem=recv.at[j, 2 * s + k, p], device_id=device, device_id_type=MESH)

    def start(when, kind, j, s, p, device):
        made = copy(kind, j, s, p, device)
        sent.append((when, made))
        if when is None:
            made.start()
        else:
            pl.when(when)(made.start)

    def arrived(j, s, parity, p):
        ref = buf.at[j, 2 * s + parity, pl.ds(p * part, part), :]
        pltpu.make_async_remote_copy(
            src_ref=ref, dst_ref=ref, send_sem=send.at[CORE, j, s, p],
            recv_sem=recv.at[j, 2 * s + parity, p], device_id=core_id,
            device_id_type=MESH).wait_recv()

    for p in range(PIECES):
        for i, device in enumerate(x_ids):
            other = device[1] // 2
            there = jnp.where(z // 2 == other, 2 * (z - 2 * other) + y, 4)
            made = pltpu.make_async_remote_copy(
                src_ref=buf.at[slot, col, pl.ds(p * part, part), :],
                dst_ref=buf.at[there, col, pl.ds(p * part, part), :],
                send_sem=send_x.at[i, p], recv_sem=recv.at[there, col, p],
                device_id=device, device_id_type=MESH)
            sent.append((None, made))
            made.start()

    def from_side(a, s, p):
        j = 2 * a + 1 - y
        arrived(j, s, k, p)
        start(a == 1 - k, CORE, j, s, p, core_id)

    far_first = (z > 2 * q).astype(jnp.int32)
    items = [
        (far_first if a == 0 else 1 - far_first, i, p)
        for a in range(2) for i in range(chips) for p in range(PIECES)
    ]
    before = []
    for a, i, p in items:
        s = lax.rem(q + i, chips)
        j = 2 * a + y
        here = z == 2 * q + a
        if i == 0:
            pl.when(jnp.logical_not(here))(functools.partial(arrived, j, s, k, p))
        else:
            arrived(j, s, k, p)
        start(has_up & (z >= 2 * q + a), UP, j, s, p, up_id)
        start(has_down & (z <= 2 * q + a), DOWN, j, s, p, down_id)
        start(None, SIDE, j, s, p, side_id)
        start(here | (a == 1 - k), CORE, j, s, p, core_id)
        before.append((a, s, p))
        if len(before) > LAG:
            from_side(*before.pop(0))

    far = jnp.logical_not(near)
    for i in range(chips):
        for p in range(PIECES):
            s = lax.rem(q + i, chips)
            if i > 0:
                pl.when(far)(functools.partial(arrived, 4, s, k, p))
            start(far, CORE, 4, s, p, core_id)
    for s in range(chips):
        for p in range(PIECES):
            arrived(slot, s, 1 - k, p)

    ones = jnp.ones((8, width), jnp.bfloat16)
    dims = (((1,), (1,)), ((), ()))
    row_degree = jnp.zeros((BLOCK, 1), jnp.float32)
    for s in range(cols):
        mine = buf[slot, s].astype(jnp.float32)
        row_degree += jnp.sum(mine * mine, axis=1, keepdims=True)
    tile = 256
    for turn in range(2):
        if turn == 1:
            for args in before:
                from_side(*args)
        other = y if turn == 0 else 1 - y
        j = 2 * k + other
        open_pair = pair_ref[row, 2 * col + other] > 0
        for t in range(BLOCK // tile):

            @pl.when(j != slot)
            def _():
                for s in range(chips):
                    for p in range(t * tile // part, (t + 1) * tile // part):
                        arrived(j, s, 1 - k, p)

            shared = jnp.zeros((BLOCK, tile), jnp.float32)
            degree = jnp.zeros((8, tile), jnp.float32)
            for s in range(cols):
                theirs = buf[j, s, t * tile:(t + 1) * tile, :]
                shared += lax.dot_general(
                    buf[slot, s], theirs, dims, preferred_element_type=jnp.float32)
                wide = theirs.astype(jnp.float32)
                square = wide * wide
                high = square.astype(jnp.bfloat16)
                low = (square - high.astype(jnp.float32)).astype(jnp.bfloat16)
                degree += lax.dot_general(ones, high, dims, preferred_element_type=jnp.float32)
                degree += lax.dot_general(ones, low, dims, preferred_element_type=jnp.float32)
            weights = shared / (row_degree + degree[:1] - shared)
            weights = jnp.where(open_pair, weights, jnp.zeros_like(weights))
            first = pl.multiple_of(other * BLOCK + t * tile, tile)
            out_ref[:, pl.ds(first, tile)] = weights.astype(jnp.bfloat16)

    for when, made in sent:
        if when is None:
            made.wait_send()
        else:
            pl.when(when)(made.wait_send)


def body(rows, cols, a_weights, tile_mask, pair_mask):
    width = a_weights.shape[1]
    chips = cols // 2
    return pl.pallas_call(
        functools.partial(kernel, rows, cols),
        out_shape=jax.ShapeDtypeStruct((BLOCK, rows // cols * BLOCK), jnp.bfloat16),
        in_specs=[
            pl.BlockSpec(memory_space=pltpu.SMEM),
            pl.BlockSpec(memory_space=pltpu.SMEM),
            pl.BlockSpec(memory_space=pltpu.VMEM),
        ],
        out_specs=pl.BlockSpec(memory_space=pltpu.VMEM),
        scratch_shapes=[
            pltpu.VMEM((5, cols, BLOCK, width), jnp.bfloat16),
            pltpu.SemaphoreType.DMA((chips - 1, PIECES)),
            pltpu.SemaphoreType.DMA((4, 5, chips, PIECES)),
            pltpu.SemaphoreType.DMA((5, cols, PIECES)),
        ],
        compiler_params=pltpu.CompilerParams(
            collective_id=0, has_side_effects=True, vmem_limit_bytes=40 * 2**20),
        cost_estimate=pl.CostEstimate(
            flops=4 * BLOCK * BLOCK * width * cols, bytes_accessed=4 * BLOCK * BLOCK,
            transcendentals=0),
    )(tile_mask, pair_mask, a_weights)


def solution(mesh):
    rows, cols = mesh.shape["row"], mesh.shape["col"]
    in_specs = (P("row", "col"), P(), P())
    out_specs = P("row", "col")
    return jax.shard_map(
        functools.partial(body, rows, cols), mesh=mesh, in_specs=in_specs,
        out_specs=out_specs, check_vma=False)
```
